32 devices in a mesh: dp: 8 (over z, y), tr: 2 (over core), tc: 2 (over x).
Axes of the slice: x: 2, y: 2, z: 4, core: 2. Of those that a mesh axis runs over, the one named last changes fastest.
Arguments:
- block_in: bfloat16 [4096, 896], P(('dp', 'tc'), 'tr'), may hold values from -6 to 6
- g_attn: float32 [896], P('tr'), may hold values from 0.5 to 1.5
- query_key_value_weight: bfloat16 [896, 1152], P('tr', 'tc'), may hold values from -0.1875 to 0.1875
- query_key_value_bias: float32 [1152], P('tc'), may hold values from -3 to 3, as said below
- output_weight: bfloat16 [896, 896], P('tr', 'tc'), may hold values from -0.75 to 0.75
- g_mlp: float32 [896], P('tr'), may hold values from 0.5 to 1.5
- w_gu: bfloat16 [2, 896, 4864], P(None, 'tr', 'tc'), may hold values from -0.1875 to 0.1875
- w_down: bfloat16 [896, 4864], P('tr', 'tc'), may hold values from -0.078125 to 0.078125
- dy: bfloat16 [4096, 896], P(('dp', 'tc'), 'tr'), may hold values from -6 to 6
Outputs:
- block_out: bfloat16 [4096, 896], P(('dp', 'tc'), 'tr')
- dx: float32 [4096, 896], P(('dp', 'tc'), 'tr')
- d_w_qkv: float32 [896, 1152], P('tr', ('tc', 'dp'))
- d_b_qkv: float32 [1152], P(('tc', 'dp'))
- d_w_o: float32 [896, 896], P('tr', ('tc', 'dp'))
- d_w_gu: float32 [2, 896, 4864], P(None, 'tr', ('tc', 'dp'))
- d_w_down: float32 [896, 4864], P('tr', ('tc', 'dp'))
- d_g_attn: float32 [896], P(('tr', 'dp'))
- d_g_mlp: float32 [896], P(('tr', 'dp'))
The draws below stay inside these ranges and needn't reach their ends.
Inputs may be any that keep to these rules, and one draw needn't show every extreme that they name: `query_key_value_bias`: biases of the query, key and value columns.
All inputs are finite; a program needn't handle non-finite values.
Results may differ from the reference program's by a relative error of at most 0.012.
Values may be sent and summed in bfloat16 or wider, within the bound.
A program may use at most 128 MiB of HBM per device.

```python
import jax
import jax.numpy as jnp
from jax import lax

D = 896
QUERY_HEADS = 14
KEY_VALUE_HEADS = 2
HEAD_SIZE = 64
FF = 4864
SEQUENCE_TOKENS = 512
C = 1152
SEQS = 8
TOKENS = 4096


def draw_query_key_value_bias(key, part):
    columns = (QUERY_HEADS + 2 * KEY_VALUE_HEADS) * HEAD_SIZE
    first = jax.random.fold_in(key, 0)
    return jnp.clip(0.5 * jax.random.normal(first, (columns,), jnp.float32), -3.0, 3.0)


def block_scale(key, extent, cuts, least, top_value):
    loudness, own = 1.0, jax.random.fold_in(key, 6)
    for position, parts in cuts:
        draws = jnp.exp(jax.random.uniform(jax.random.fold_in(own, position), (parts,), jnp.float32, least / len(cuts), top_value / len(cuts)))
        loudness = loudness * jnp.repeat(draws, extent[position] // parts).reshape([-1 if axis == position else 1 for axis in range(len(extent))])
    return loudness


def bell_draw(own_key, extent, spread, reach, shards=(), kind=jnp.bfloat16):
    values = jax.random.normal(own_key, extent, jnp.float32) * spread
    if len(shards) > 0:
        values = block_scale(own_key, extent, shards, -0.22, 0.18) * values
    return jnp.clip(values, min=-reach, max=reach).astype(kind)


def setup_inputs(seed: int = 0) -> dict:
    splits = jax.random.split(jax.random.key(seed), 10)
    block_in = bell_draw(splits[0], (TOKENS, D), 1.0, 6.0, ((0, 16), (1, 2)))
    g_attn = jnp.clip(1.0 + 0.1 * jax.random.normal(splits[1], (D,), jnp.float32), 0.5, 1.5)
    query_key_value_weight = bell_draw(splits[2], (D, C), D ** -0.5, 0.1875, ((0, 2), (1, 2)))
    query_key_value_bias = draw_query_key_value_bias(jax.random.fold_in(splits[9], 71), 0)
    output_weight = bell_draw(splits[4], (D, QUERY_HEADS * HEAD_SIZE), (QUERY_HEADS * HEAD_SIZE // 16) ** -0.5, 0.75, ((0, 2), (1, 2)))
    g_mlp = jnp.clip(1.0 + 0.1 * jax.random.normal(splits[5], (D,), jnp.float32), 0.5, 1.5)
    w_gu = bell_draw(splits[6], (2, D, FF), D ** -0.5, 0.1875, ((1, 2), (2, 2)))
    w_down = bell_draw(splits[7], (D, FF), FF ** -0.5, 0.078125, ((0, 2), (1, 2)))
    dy = bell_draw(splits[8], (TOKENS, D), 1.0, 6.0, ((0, 16), (1, 2)))
    return {"block_in": block_in, "g_attn": g_attn, "query_key_value_weight": query_key_value_weight, "query_key_value_bias": query_key_value_bias, "output_weight": output_weight, "g_mlp": g_mlp, "w_gu": w_gu, "w_down": w_down, "dy": dy}


EPS = 1e-06
ROPE_BASE = 1000000.0

def rotate_half(value):
    half = value.shape[-1] // 2
    return jnp.concatenate([-value[..., half:], value[..., :half]], axis=-1)

def rope_tables(count, head_index):
    half = head_index // 2
    inverse = ROPE_BASE ** (-jnp.arange(half, dtype=jnp.float32) * 2.0 / head_index)
    angle = jnp.arange(count).astype(jnp.float32)[:, None] * inverse[None, :]
    angle = jnp.concatenate([angle, angle], axis=1)
    return (jnp.cos(angle), jnp.sin(angle))

def rope_apply(value, cosv, sinv):
    return value * cosv + rotate_half(value) * sinv

def rope_back(value, cosv, sinv):
    return value * cosv - rotate_half(value * sinv)

def one_sequence(block_in, g_attn, query_key_value_weight, query_key_value_bias, output_weight, g_mlp, w_gu, w_down, dy):
    single_float_type = jnp.float32
    bfloat_type = jnp.bfloat16
    head_group = QUERY_HEADS // KEY_VALUE_HEADS
    scale = HEAD_SIZE ** (-0.5)
    xf = block_in.astype(single_float_type)
    r1 = lax.rsqrt(lax.optimization_barrier(jnp.mean(xf * xf, axis=1, keepdims=True)) + EPS)
    first_normed_input = (xf * r1 * g_attn).astype(bfloat_type)
    query_key_value = (jnp.dot(first_normed_input, query_key_value_weight, preferred_element_type=single_float_type) + query_key_value_bias).reshape(SEQUENCE_TOKENS, KEY_VALUE_HEADS, head_group + 2, HEAD_SIZE)
    cosv, sinv = rope_tables(SEQUENCE_TOKENS, HEAD_SIZE)
    query = rope_apply(query_key_value[:, :, :head_group], cosv[:, None, None], sinv[:, None, None]).astype(bfloat_type)
    keys = rope_apply(query_key_value[:, :, head_group], cosv[:, None], sinv[:, None]).astype(bfloat_type)
    values = query_key_value[:, :, head_group + 1].astype(bfloat_type)
    place = jnp.arange(SEQUENCE_TOKENS)
    allowed = place[:, None] >= place[None, :]
    scores = jnp.einsum('tkgd,skd->kgts', query.astype(single_float_type), keys.astype(single_float_type)) * scale
    scores = jnp.where(allowed, scores, -1e+30)
    top = lax.optimization_barrier(jnp.max(scores, axis=3, keepdims=True))
    lse = top + jnp.log(lax.optimization_barrier(jnp.sum(jnp.exp(scores - top), axis=3, keepdims=True)))
    prob = jnp.exp(scores - lse)
    prob_b = prob.astype(bfloat_type)
    attn = jnp.einsum('kgts,skd->tkgd', prob_b.astype(single_float_type), values.astype(single_float_type)).astype(bfloat_type)
    attn_flat = attn.reshape(SEQUENCE_TOKENS, QUERY_HEADS * HEAD_SIZE)
    h1 = xf + jnp.dot(attn_flat, output_weight.T, preferred_element_type=single_float_type)
    r2 = lax.rsqrt(lax.optimization_barrier(jnp.mean(h1 * h1, axis=1, keepdims=True)) + EPS)
    xn2 = (h1 * r2 * g_mlp).astype(bfloat_type)
    gate = jnp.dot(xn2, w_gu[0], preferred_element_type=single_float_type)
    upper = jnp.dot(xn2, w_gu[1], preferred_element_type=single_float_type)
    sig = jax.nn.sigmoid(gate)
    silu_v = gate * sig
    mixed = (silu_v * upper).astype(bfloat_type)
    block_out = (h1 + jnp.dot(mixed, w_down.T, preferred_element_type=single_float_type)).astype(bfloat_type)
    dyf = dy.astype(single_float_type)
    d_w_down = jnp.dot(dy.T, mixed, preferred_element_type=single_float_type)
    dmixed = jnp.dot(dy, w_down, preferred_element_type=single_float_type)
    dgate = (dmixed * upper * sig * (1.0 + gate * (1.0 - sig))).astype(bfloat_type)
    dup = (dmixed * silu_v).astype(bfloat_type)
    d_w_gu = jnp.stack([jnp.dot(xn2.T, dgate, preferred_element_type=single_float_type), jnp.dot(xn2.T, dup, preferred_element_type=single_float_type)])
    dxn2 = jnp.dot(dgate, w_gu[0].T, preferred_element_type=single_float_type) + jnp.dot(dup, w_gu[1].T, preferred_element_type=single_float_type)
    d_g_mlp = lax.optimization_barrier(jnp.sum(dxn2 * h1 * r2, axis=0))
    scaled = g_mlp * dxn2
    dh1 = dyf + r2 * scaled - h1 * r2 ** 3 * lax.optimization_barrier(jnp.mean(scaled * h1, axis=1, keepdims=True))
    hidden_gradient_block = dh1.astype(bfloat_type)
    d_w_o = jnp.dot(hidden_gradient_block.T, attn_flat, preferred_element_type=single_float_type)
    attention_gradient = jnp.dot(hidden_gradient_block, output_weight, preferred_element_type=single_float_type).astype(bfloat_type).reshape(SEQUENCE_TOKENS, KEY_VALUE_HEADS, head_group, HEAD_SIZE)
    delta = jnp.transpose(lax.optimization_barrier(jnp.sum(attention_gradient.astype(single_float_type) * attn.astype(single_float_type), axis=3)), (1, 2, 0))[..., None]
    dprob = jnp.einsum('tkgd,skd->kgts', attention_gradient.astype(single_float_type), values.astype(single_float_type))
    dscore = (prob * (dprob - delta) * scale).astype(bfloat_type)
    dquery = jnp.einsum('kgts,skd->tkgd', dscore.astype(single_float_type), keys.astype(single_float_type))
    dkeys = jnp.einsum('kgts,tkgd->skd', dscore.astype(single_float_type), query.astype(single_float_type))
    dvalues = jnp.einsum('kgts,tkgd->skd', prob_b.astype(single_float_type), attention_gradient.astype(single_float_type))
    dquery = rope_back(dquery, cosv[:, None, None], sinv[:, None, None])
    dkeys = rope_back(dkeys, cosv[:, None], sinv[:, None])
    dqkv = jnp.concatenate([dquery, dkeys[:, :, None], dvalues[:, :, None]], axis=2).reshape(SEQUENCE_TOKENS, C)
    d_b_qkv = lax.optimization_barrier(jnp.sum(dqkv, axis=0))
    dqkv_b = dqkv.astype(bfloat_type)
    d_w_qkv = jnp.dot(first_normed_input.T, dqkv_b, preferred_element_type=single_float_type)
    dxn1 = jnp.dot(dqkv_b, query_key_value_weight.T, preferred_element_type=single_float_type)
    d_g_attn = lax.optimization_barrier(jnp.sum(dxn1 * xf * r1, axis=0))
    scaled = g_attn * dxn1
    dx = dh1 + r1 * scaled - xf * r1 ** 3 * lax.optimization_barrier(jnp.mean(scaled * xf, axis=1, keepdims=True))
    return (block_out, dx, (d_w_qkv, d_b_qkv, d_w_o, d_w_gu, d_w_down, d_g_attn, d_g_mlp))

def reference(block_in, g_attn, query_key_value_weight, query_key_value_bias, output_weight, g_mlp, w_gu, w_down, dy):
    single_float_type = jnp.float32
    start = (jnp.zeros((D, C), single_float_type), jnp.zeros((C,), single_float_type), jnp.zeros((D, QUERY_HEADS * HEAD_SIZE), single_float_type), jnp.zeros((2, D, FF), single_float_type), jnp.zeros((D, FF), single_float_type), jnp.zeros((D,), single_float_type), jnp.zeros((D,), single_float_type))

    def step(carry, pieces):
        block_out, dx, grads = one_sequence(pieces[0], g_attn, query_key_value_weight, query_key_value_bias, output_weight, g_mlp, w_gu, w_down, pieces[1])
        carry = tuple((total + part for total, part in zip(carry, grads)))
        return (carry, (block_out, dx))
    grads, outs = lax.scan(step, start, (block_in.reshape(SEQS, SEQUENCE_TOKENS, D), dy.reshape(SEQS, SEQUENCE_TOKENS, D)))
    block_out = outs[0].reshape(TOKENS, D)
    dx = outs[1].reshape(TOKENS, D)
    return (block_out, dx, grads[0], grads[1], grads[2], grads[3], grads[4], grads[5], grads[6])
```

```python
import jax
import jax.numpy as jnp
from jax import lax
from jax.sharding import PartitionSpec as P

QUERY_HEADS = 14
KEY_VALUE_HEADS = 2
HEAD_SIZE = 64
SEQUENCE_TOKENS = 512


EPS = 1e-06
ROPE_BASE = 1000000.0


def rotate_half(value):
    half = value.shape[-1] // 2
    return jnp.concatenate([-value[..., half:], value[..., :half]], axis=-1)


def rope_tables(positions, head_index):
    half = head_index // 2
    inverse = ROPE_BASE ** (-jnp.arange(half, dtype=jnp.float32) * 2.0 / head_index)
    angle = positions.astype(jnp.float32)[:, None] * inverse[None, :]
    angle = jnp.concatenate([angle, angle], axis=1)
    return (jnp.cos(angle), jnp.sin(angle))


def rope_apply(value, cosv, sinv):
    return value * cosv + rotate_half(value) * sinv


def rope_back(value, cosv, sinv):
    return value * cosv - rotate_half(value * sinv)


def contract_last(left, right):
    return lax.dot_general(
        left, right, (((1,), (1,)), ((), ())), preferred_element_type=jnp.float32
    )


def contract_first(left, right):
    return lax.dot_general(
        left, right, (((0,), (0,)), ((), ())), preferred_element_type=jnp.float32
    )


def row_total(values):
    return lax.psum(values, "tr")


def width_rows(values):
    return lax.all_gather(values, "tc", axis=0, tiled=True)


def width_sums(term, rows):
    return lax.psum_scatter(
        term(jnp.int32(0), lax.axis_size("tc") * rows), "tc", scatter_dimension=0, tiled=True
    )


def pair_rows(values):
    return lax.all_gather(values, "tr", axis=0, tiled=True)


def pair_sums(term, rows):
    return lax.psum_scatter(
        term(jnp.int32(0), lax.axis_size("tr") * rows), "tr", scatter_dimension=0, tiled=True
    )


def swapped(values, axis, bit):
    size = lax.axis_size(axis)
    return lax.ppermute(values, axis, [(i, i ^ bit) for i in range(size)])


def scatter_sum(grad, first):
    size = lax.axis_size("dp")
    bits = size.bit_length() - 1
    me = lax.axis_index("dp")
    lead = grad.shape[0]
    value = grad.reshape((lead,) + (2,) * bits + (grad.shape[1] // size, grad.shape[2]))
    order = list(range(bits))
    if first == 1 and bits > 1:
        order[0], order[1] = 1, 0
    left = list(range(bits))[::-1]
    for step, bit in enumerate(order):
        dim = 1 + left.index(bit)
        mine = lax.rem(me // (1 << bit), 2)
        keep = lax.dynamic_index_in_dim(value, mine, dim, keepdims=False)
        send = lax.dynamic_index_in_dim(value, 1 - mine, dim, keepdims=False)
        got = swapped(send, "dp", 1 << bit)
        value = keep.astype(jnp.float32) + got.astype(jnp.float32)
        if step < bits - 1:
            value = value.astype(jnp.bfloat16)
        left.remove(bit)
    return value


def grad_block(left, right, first):
    grad = contract_first(left, right).astype(jnp.bfloat16)
    return scatter_sum(grad[None], first)[0].T


def attend(query, keys, values, qpos, kpos):
    scale = query.shape[-1] ** (-0.5)
    scores = jnp.einsum("tkgd,skd->kgts", query, keys, preferred_element_type=jnp.float32) * scale
    scores = jnp.where(qpos[:, None] >= kpos[None, :], scores, -1e30)
    top = jnp.max(scores, axis=3, keepdims=True)
    lse = top + jnp.log(jnp.sum(jnp.exp(scores - top), axis=3, keepdims=True))
    prob = jnp.exp(scores - lse).astype(jnp.bfloat16)
    output = jnp.einsum("kgts,skd->tkgd", prob, values, preferred_element_type=jnp.float32).astype(
        jnp.bfloat16
    )
    return (output, lse)


def attend_back(query, keys, values, output, dout, lse, qpos, kpos):
    scale = query.shape[-1] ** (-0.5)
    scores = jnp.einsum("tkgd,skd->kgts", query, keys, preferred_element_type=jnp.float32) * scale
    scores = jnp.where(qpos[:, None] >= kpos[None, :], scores, -1e30)
    prob = jnp.exp(scores - lse)
    prob_b = prob.astype(jnp.bfloat16)
    delta = jnp.transpose(
        jnp.sum(dout.astype(jnp.float32) * output.astype(jnp.float32), axis=3), (1, 2, 0)
    )[..., None]
    dprob = jnp.einsum("tkgd,skd->kgts", dout, values, preferred_element_type=jnp.float32)
    dscore = (prob * (dprob - delta) * scale).astype(jnp.bfloat16)
    dquery = jnp.einsum("kgts,skd->tkgd", dscore, keys, preferred_element_type=jnp.float32)
    dkeys = jnp.einsum("kgts,tkgd->skd", dscore, query, preferred_element_type=jnp.float32)
    dvalues = jnp.einsum("kgts,tkgd->skd", prob_b, dout, preferred_element_type=jnp.float32)
    return (dquery, dkeys, dvalues)


def per_device(
    block_in,
    g_attn,
    query_key_value_weight,
    query_key_value_bias,
    output_weight,
    g_mlp,
    w_gu,
    w_down,
    dy,
):
    single_float_type = jnp.float32
    bfloat_type = jnp.bfloat16
    rows = block_in.shape[0]
    model_width = block_in.shape[1] * lax.axis_size("tr")
    head_group = QUERY_HEADS // KEY_VALUE_HEADS
    heads_kv = query_key_value_weight.shape[1] // ((head_group + 2) * HEAD_SIZE)
    block = rows * lax.axis_size("tc")
    xf = block_in.astype(single_float_type)
    r1 = lax.rsqrt(row_total(jnp.sum(xf * xf, axis=1)) / model_width + EPS)[:, None]
    first_normed_input = (xf * r1 * g_attn).astype(bfloat_type)
    xn1_all = width_rows(first_normed_input)

    def qkv_forward(start, count):
        return jnp.dot(xn1_all, query_key_value_weight, preferred_element_type=single_float_type)

    query_key_value = pair_sums(qkv_forward, rows) + query_key_value_bias
    query_key_value = query_key_value.reshape(rows, heads_kv, head_group + 2, HEAD_SIZE)
    first = lax.axis_index("tr") * rows
    cosv, sinv = rope_tables((first + jnp.arange(rows)) % SEQUENCE_TOKENS, HEAD_SIZE)
    query = rope_apply(
        query_key_value[:, :, :head_group], cosv[:, None, None], sinv[:, None, None]
    ).astype(bfloat_type)
    keys = rope_apply(query_key_value[:, :, head_group], cosv[:, None], sinv[:, None]).astype(
        bfloat_type
    )
    values = query_key_value[:, :, head_group + 1].astype(bfloat_type)
    kv_here = jnp.stack([keys, values], axis=2).reshape(rows, heads_kv * 2 * HEAD_SIZE)
    kv_all = pair_rows(kv_here).reshape(block, heads_kv, 2, HEAD_SIZE)
    seqs = max(rows // SEQUENCE_TOKENS, 1)
    qlen = min(rows, SEQUENCE_TOKENS)
    q_own = query.reshape(seqs, qlen, heads_kv, head_group, HEAD_SIZE)
    k_own = kv_all[:, :, 0].reshape(seqs, SEQUENCE_TOKENS, heads_kv, HEAD_SIZE)
    v_own = kv_all[:, :, 1].reshape(seqs, SEQUENCE_TOKENS, heads_kv, HEAD_SIZE)
    qpos = first + jnp.arange(qlen)
    kpos = jnp.arange(SEQUENCE_TOKENS)

    def forward_one(pieces):
        return attend(pieces[0], pieces[1], pieces[2], qpos, kpos)

    o_own, lse = lax.map(forward_one, (q_own, k_own, v_own))
    o_all = pair_rows(o_own.reshape(rows, heads_kv * head_group * HEAD_SIZE))

    def attn_term(start, count):
        return contract_last(o_all, output_weight)

    h1 = xf + width_sums(attn_term, rows)
    r2 = lax.rsqrt(row_total(jnp.sum(h1 * h1, axis=1)) / model_width + EPS)[:, None]
    xn2 = (h1 * r2 * g_mlp).astype(bfloat_type)
    xn2_all = width_rows(xn2)

    def gate_term(start, count):
        return jnp.einsum("td,gdf->tgf", xn2_all, w_gu, preferred_element_type=single_float_type)

    gate_up = pair_sums(gate_term, rows)
    gate = gate_up[:, 0]
    upper = gate_up[:, 1]
    sig = jax.nn.sigmoid(gate)
    silu_v = gate * sig
    mixed = (silu_v * upper).astype(bfloat_type)
    mixed_all = pair_rows(mixed)

    def down_term(start, count):
        return contract_last(mixed_all, w_down)

    block_out = (h1 + width_sums(down_term, rows)).astype(bfloat_type)
    dyf = dy.astype(single_float_type)
    dy_all = width_rows(dy)
    d_w_down = grad_block(mixed_all, dy_all, 0)

    def hidden_term(start, count):
        return jnp.dot(dy_all, w_down, preferred_element_type=single_float_type)

    dmixed = pair_sums(hidden_term, rows)
    dgate = dmixed * upper * sig * (1.0 + gate * (1.0 - sig))
    dup = dmixed * silu_v
    dgu = jnp.stack([dgate, dup], axis=1).astype(bfloat_type)
    dgu_all = pair_rows(dgu)
    d_w_gu = jnp.stack([grad_block(dgu_all[:, 0], xn2_all, 1), grad_block(dgu_all[:, 1], xn2_all, 0)])

    def input_term(start, count):
        return jnp.einsum("tgf,gdf->td", dgu_all, w_gu, preferred_element_type=single_float_type)

    dxn2 = width_sums(input_term, rows)
    d_g_mlp = jnp.sum(dxn2 * h1 * r2, axis=0)
    scaled = g_mlp * dxn2
    dh1 = (
        dyf
        + r2 * scaled
        - h1 * r2**3 * row_total(jnp.sum(scaled * h1, axis=1))[:, None] / model_width
    )
    hidden_gradient_block = dh1.astype(bfloat_type)
    dh1_all = width_rows(hidden_gradient_block)
    d_w_o = grad_block(o_all, dh1_all, 1)

    def head_term(start, count):
        return jnp.dot(dh1_all, output_weight, preferred_element_type=single_float_type)

    dout = pair_sums(head_term, rows).astype(bfloat_type)
    dout = dout.reshape(seqs, qlen, heads_kv, head_group, HEAD_SIZE)

    def backward_one(pieces):
        return attend_back(
            pieces[0], pieces[1], pieces[2], pieces[3], pieces[4], pieces[5], qpos, kpos
        )

    dquery, dkeys, dvalues = lax.map(backward_one, (q_own, k_own, v_own, o_own, dout, lse))
    kv_grad = jnp.stack([dkeys, dvalues], axis=3).reshape(
        seqs * SEQUENCE_TOKENS, heads_kv, 2, HEAD_SIZE
    )
    kv_part = kv_grad
    kv_part = kv_part.reshape(block, heads_kv * 2 * HEAD_SIZE)

    def kv_term(start, count):
        return kv_part

    kv_back = pair_sums(kv_term, rows).reshape(rows, heads_kv, 2, HEAD_SIZE)
    q_back = rope_back(
        dquery.reshape(rows, heads_kv, head_group, HEAD_SIZE),
        cosv[:, None, None],
        sinv[:, None, None],
    )
    k_back = rope_back(kv_back[:, :, 0], cosv[:, None], sinv[:, None])
    dqkv = jnp.concatenate(
        [q_back, k_back[:, :, None], kv_back[:, :, 1][:, :, None]], axis=2
    ).reshape(rows, -1)
    bias_part = jnp.sum(dqkv, axis=0)
    dqkv_all = pair_rows(dqkv.astype(bfloat_type))
    d_w_qkv = grad_block(dqkv_all, xn1_all, 0)

    def qkv_term(start, count):
        return contract_last(dqkv_all, query_key_value_weight)

    dxn1 = width_sums(qkv_term, rows)
    d_g_attn = jnp.sum(dxn1 * xf * r1, axis=0)
    scaled = g_attn * dxn1
    stats = row_total((jnp.sum(scaled * xf, axis=1), bias_part))
    d_b_qkv = stats[1]
    dx = dh1 + r1 * scaled - xf * r1**3 * stats[0][:, None] / model_width
    gains = lax.psum((d_g_attn, d_g_mlp), "tc")
    grads = (
        d_w_qkv,
        lax.psum_scatter(d_b_qkv, "dp", scatter_dimension=0, tiled=True),
        d_w_o,
        d_w_gu,
        d_w_down,
        lax.psum_scatter(gains[0], "dp", scatter_dimension=0, tiled=True),
        lax.psum_scatter(gains[1], "dp", scatter_dimension=0, tiled=True),
    )
    return (block_out, dx, grads[0], grads[1], grads[2], grads[3], grads[4], grads[5], grads[6])


def solution(mesh):
    placed = (
        P(("dp", "tc"), "tr"),
        P("tr"),
        P("tr", "tc"),
        P("tc"),
        P("tr", "tc"),
        P("tr"),
        P(None, "tr", "tc"),
        P("tr", "tc"),
        P(("dp", "tc"), "tr"),
    )
    return jax.shard_map(
        per_device,
        mesh=mesh,
        in_specs=placed,
        out_specs=(
            P(("dp", "tc"), "tr"),
            P(("dp", "tc"), "tr"),
            P("tr", ("tc", "dp")),
            P(("tc", "dp")),
            P("tr", ("tc", "dp")),
            P(None, "tr", ("tc", "dp")),
            P("tr", ("tc", "dp")),
            P(("tr", "dp")),
            P(("tr", "dp")),
        ),
        check_vma=False,
    )
```

```python
import jax
import jax.numpy as jnp
from jax import lax
from jax.sharding import PartitionSpec as P

QUERY_HEADS = 14
KEY_VALUE_HEADS = 2
HEAD_SIZE = 64
SEQUENCE_TOKENS = 512


EPS = 1e-06
ROPE_BASE = 1000000.0


def rotate_half(value):
    half = value.shape[-1] // 2
    return jnp.concatenate([-value[..., half:], value[..., :half]], axis=-1)


def rope_tables(positions, head_index):
    half = head_index // 2
    inverse = ROPE_BASE ** (-jnp.arange(half, dtype=jnp.float32) * 2.0 / head_index)
    angle = positions.astype(jnp.float32)[:, None] * inverse[None, :]
    angle = jnp.concatenate([angle, angle], axis=1)
    return (jnp.cos(angle), jnp.sin(angle))


def rope_apply(value, cosv, sinv):
    return value * cosv + rotate_half(value) * sinv


def rope_back(value, cosv, sinv):
    return value * cosv - rotate_half(value * sinv)


def contract_last(left, right):
    return lax.dot_general(
        left, right, (((1,), (1,)), ((), ())), preferred_element_type=jnp.float32
    )


def contract_first(left, right):
    return lax.dot_general(
        left, right, (((0,), (0,)), ((), ())), preferred_element_type=jnp.float32
    )


def swapped(values, axis, bit=1):
    size = lax.axis_size(axis)
    return lax.ppermute(values, axis, [(i, i ^ bit) for i in range(size)])


def tie(*values):
    return lax.optimization_barrier(values)


def with_rows(values, axis):
    return jnp.concatenate([values, swapped(values, axis)], axis=0)


def sum_rows(values, axis):
    rows = values.shape[0] // 2
    send = values[rows:].astype(jnp.bfloat16)
    return values[:rows].astype(jnp.float32) + swapped(send, axis).astype(jnp.float32)


def two_halves(values, axis, first):
    half = values.shape[axis] // 2
    low = lax.slice_in_dim(values, 0, half, axis=axis)
    high = lax.slice_in_dim(values, half, 2 * half, axis=axis)
    return (jnp.where(first, low, high), jnp.where(first, high, low))


def joined(mine, other, axis, first):
    return jnp.where(
        first,
        jnp.concatenate([mine, other], axis=axis),
        jnp.concatenate([other, mine], axis=axis),
    )


def exchange_bit(value, dim, bit):
    mine = lax.rem(lax.axis_index("dp") // (1 << bit), 2)
    keep = lax.dynamic_index_in_dim(value, mine, dim, keepdims=False)
    send = lax.dynamic_index_in_dim(value, 1 - mine, dim, keepdims=False)
    return (keep, send)


def scatter_start(grad, bits, flip):
    value = grad.reshape((2,) * bits + (grad.shape[0] >> bits, grad.shape[1]))
    order = list(range(bits))
    if flip and bits > 1:
        order[0], order[1] = 1, 0
    if bits == 0:
        return (value, None, order)
    keep, send = exchange_bit(value, bits - 1 - order[0], order[0])
    return (keep, send, order)


def scatter_finish(keep, send, order):
    bits = len(order)
    left = list(range(bits))[::-1]
    for step, bit in enumerate(order):
        if step > 0:
            keep, send = exchange_bit(value, left.index(bit), bit)
        got = swapped(send, "dp", 1 << bit)
        value = keep.astype(jnp.float32) + got.astype(jnp.float32)
        value = value.astype(jnp.bfloat16) if step < bits - 1 else value
        left.remove(bit)
    return value if bits else keep


def last_bit(own, other, top):
    which = (lax.axis_index("dp") // (1 << top)) == lax.axis_index("tr")
    keep = jnp.where(which, own, other)
    send = jnp.where(which, other, own).astype(jnp.bfloat16)
    return keep.astype(jnp.float32) + swapped(send, "dp", 1 << top).astype(jnp.float32)


def product(left, right):
    return contract_first(left, right).astype(jnp.bfloat16)


def attend(query, keys, values, qpos, kpos):
    scale = query.shape[-1] ** (-0.5)
    scores = jnp.einsum("tkgd,skd->kgts", query, keys, preferred_element_type=jnp.float32) * scale
    scores = jnp.where(qpos[:, None] >= kpos[None, :], scores, -1e30)
    top = jnp.max(scores, axis=3, keepdims=True)
    lse = top + jnp.log(jnp.sum(jnp.exp(scores - top), axis=3, keepdims=True))
    prob = jnp.exp(scores - lse).astype(jnp.bfloat16)
    output = jnp.einsum("kgts,skd->tkgd", prob, values, preferred_element_type=jnp.float32).astype(
        jnp.bfloat16
    )
    return (output, lse)


def attend_back(query, keys, values, output, dout, lse, qpos, kpos):
    scale = query.shape[-1] ** (-0.5)
    scores = jnp.einsum("tkgd,skd->kgts", query, keys, preferred_element_type=jnp.float32) * scale
    scores = jnp.where(qpos[:, None] >= kpos[None, :], scores, -1e30)
    prob = jnp.exp(scores - lse)
    prob_b = prob.astype(jnp.bfloat16)
    delta = jnp.transpose(
        jnp.sum(dout.astype(jnp.float32) * output.astype(jnp.float32), axis=3), (1, 2, 0)
    )[..., None]
    dprob = jnp.einsum("tkgd,skd->kgts", dout, values, preferred_element_type=jnp.float32)
    dscore = (prob * (dprob - delta) * scale).astype(jnp.bfloat16)
    dquery = jnp.einsum("kgts,skd->tkgd", dscore, keys, preferred_element_type=jnp.float32)
    dkeys = jnp.einsum("kgts,tkgd->skd", dscore, query, preferred_element_type=jnp.float32)
    dvalues = jnp.einsum("kgts,tkgd->skd", prob_b, dout, preferred_element_type=jnp.float32)
    return (dquery, dkeys, dvalues)


def per_device(
    block_in,
    g_attn,
    query_key_value_weight,
    query_key_value_bias,
    output_weight,
    g_mlp,
    w_gu,
    w_down,
    dy,
):
    f32 = jnp.float32
    bf16 = jnp.bfloat16
    n_dp = lax.axis_size("dp")
    bits = n_dp.bit_length() - 1
    first = lax.axis_index("tr") == 0
    head_group = QUERY_HEADS // KEY_VALUE_HEADS
    heads_kv = query_key_value_weight.shape[1] // ((head_group + 2) * HEAD_SIZE)
    qkv_columns = query_key_value_weight.shape[1]
    head_columns = output_weight.shape[1]
    width = block_in.shape[1]
    model_width = 2 * width
    seqs = block_in.shape[0] * 2 // SEQUENCE_TOKENS
    quarter = SEQUENCE_TOKENS // 4
    rows = seqs * quarter
    assert lax.axis_size("tr") == 2 and lax.axis_size("tc") == 2 and seqs == 1

    x_mine, x_other = two_halves(jnp.stack([block_in, dy]), 1, first)
    x_full = joined(x_mine, swapped(x_other, "tr"), 2, first)
    gains = lax.all_gather(jnp.stack([g_attn, g_mlp]), "tr", axis=1, tiled=True)
    gain_a, gain_m = gains[0], gains[1]
    xf = x_full[0].astype(f32)
    r1 = lax.rsqrt(jnp.sum(xf * xf, axis=1, keepdims=True) / model_width + EPS)
    xn1 = (xf * r1 * gain_a).astype(bf16)
    w_qkv = lax.all_gather(query_key_value_weight, "tr", axis=0, tiled=True)
    xn1_pair = with_rows(xn1, "tc")
    xn1_all = with_rows(xn1_pair, "tr")

    tr = lax.axis_index("tr")
    tc = lax.axis_index("tc")
    places = jnp.arange(quarter)
    starts = [
        tc * 2 * quarter + tr * quarter,
        (1 - tc) * 2 * quarter + tr * quarter,
        tc * 2 * quarter + (1 - tr) * quarter,
        (1 - tc) * 2 * quarter + (1 - tr) * quarter,
    ]
    kpos = jnp.concatenate([start + places for start in starts])
    qpos = kpos[: 2 * quarter]
    cosv, sinv = rope_tables(kpos, HEAD_SIZE)
    qkv = jnp.dot(xn1_all, w_qkv, preferred_element_type=f32) + query_key_value_bias
    qkv = qkv.reshape(4 * rows, heads_kv, head_group + 2, HEAD_SIZE)
    cos_q, sin_q = cosv[: 2 * rows], sinv[: 2 * rows]
    query = rope_apply(
        qkv[: 2 * rows, :, :head_group], cos_q[:, None, None], sin_q[:, None, None]
    ).astype(bf16)
    keys = rope_apply(qkv[:, :, head_group], cosv[:, None], sinv[:, None]).astype(bf16)
    values = qkv[:, :, head_group + 1].astype(bf16)
    output, lse = attend(query, keys, values, qpos, kpos)
    o_pair = output.reshape(2 * rows, head_columns)
    w_o = lax.all_gather(output_weight, "tr", axis=0, tiled=True)
    h1 = xf + sum_rows(contract_last(o_pair, w_o), "tc")

    gu_mine, gu_other = two_halves(w_gu, 2, first)
    wgu = joined(gu_mine, swapped(gu_other, "tr"), 1, first)
    down_mine, down_other = two_halves(w_down, 1, first)
    wdown = joined(down_mine, swapped(down_other, "tr"), 0, first)
    dy_all = with_rows(with_rows(x_full[1], "tc"), "tr")
    dmixed = jnp.dot(dy_all, wdown, preferred_element_type=f32)

    r2 = lax.rsqrt(jnp.sum(h1 * h1, axis=1, keepdims=True) / model_width + EPS)
    xn2 = (h1 * r2 * gain_m).astype(bf16)
    xn2_all = with_rows(with_rows(xn2, "tc"), "tr")
    gate = jnp.dot(xn2_all, wgu[0], preferred_element_type=f32)
    upper = jnp.dot(xn2_all, wgu[1], preferred_element_type=f32)
    sig = jax.nn.sigmoid(gate)
    silu_v = gate * sig
    mixed = (silu_v * upper).astype(bf16)
    dgate = (dmixed * upper * sig * (1.0 + gate * (1.0 - sig))).astype(bf16)
    dup = (dmixed * silu_v).astype(bf16)

    dy_own, dy_sib = two_halves(dy_all, 1, first)
    xn2_own, xn2_sib = two_halves(xn2_all, 1, first)
    pairs = [(mixed, dy_own, dy_sib), (dgate, xn2_own, xn2_sib), (dup, xn2_own, xn2_sib)]
    others = [product(left, sib) for left, own, sib in pairs]
    started = [scatter_start(product(left, own), bits - 1, False) for left, own, sib in pairs]
    tied = tie(dgate, dup, mixed, *others, *[item[1] for item in started])
    dgate, dup, mixed = tied[:3]
    others = tied[3:6]
    sends = tied[6:]
    own_sums = [
        scatter_finish(item[0], send, item[2]) for item, send in zip(started, sends)
    ]
    other_sums = [
        scatter_finish(*scatter_start(swapped(other, "tr"), bits - 1, True)) for other in others
    ]
    hidden_sums = [
        last_bit(own, other, bits - 1).T for own, other in zip(own_sums, other_sums)
    ]
    d_w_down = hidden_sums[0]
    d_w_gu = jnp.stack(hidden_sums[1:])

    dxn2 = sum_rows(
        sum_rows(contract_last(dgate, wgu[0]) + contract_last(dup, wgu[1]), "tr"), "tc"
    )
    d_g_mlp = jnp.sum(dxn2 * h1 * r2, axis=0)
    scaled = gain_m * dxn2
    dh1 = (
        x_full[1].astype(f32)
        + r2 * scaled
        - h1 * r2**3 * (jnp.sum(scaled * h1, axis=1, keepdims=True) / model_width)
    )
    dh1_pair = with_rows(dh1.astype(bf16), "tc")
    dout = jnp.dot(dh1_pair, w_o, preferred_element_type=f32).astype(bf16)
    dout = dout.reshape(2 * rows, heads_kv, head_group, HEAD_SIZE)
    dquery, dkeys, dvalues = attend_back(
        query, keys, values, output, dout, lse, qpos, kpos
    )
    kv_part = jnp.stack([dkeys, dvalues], axis=2).reshape(4 * rows, heads_kv * 2 * HEAD_SIZE)
    kv_back = sum_rows(kv_part, "tr").reshape(2 * rows, heads_kv, 2, HEAD_SIZE)
    q_back = rope_back(dquery, cos_q[:, None, None], sin_q[:, None, None])
    k_back = rope_back(kv_back[:, :, 0], cos_q[:, None], sin_q[:, None])
    dqkv = jnp.concatenate(
        [q_back, k_back[:, :, None], kv_back[:, :, 1][:, :, None]], axis=2
    ).reshape(2 * rows, qkv_columns)
    bias_part = jnp.sum(dqkv, axis=0)
    dqkvb = dqkv.astype(bf16)
    dxn1 = sum_rows(contract_last(dqkvb, w_qkv), "tc")

    def pair_grad(left, right, flip):
        own, sib = two_halves(right, 1, first)
        got = swapped(product(left, sib), "tr")
        total = (contract_first(left, own) + got.astype(f32)).astype(bf16)
        return scatter_finish(*scatter_start(total, bits, flip)).T

    d_w_o = pair_grad(o_pair, dh1_pair, False)
    d_w_qkv = pair_grad(dqkvb, xn1_pair, True)

    d_g_attn = jnp.sum(dxn1 * xf * r1, axis=0)
    scaled = gain_a * dxn1
    dx = (
        dh1
        + r1 * scaled
        - xf * r1**3 * (jnp.sum(scaled * xf, axis=1, keepdims=True) / model_width)
    )

    mlp_out = sum_rows(sum_rows(contract_last(mixed, wdown), "tr"), "tc")
    block_out = (h1 + mlp_out).astype(bf16)

    def placed(full):
        own, sib = two_halves(full, 1, first)
        return joined(own, swapped(sib, "tr"), 0, first)

    gain_parts = jnp.stack([d_g_attn, d_g_mlp]).reshape(2, 2, n_dp, width // n_dp)
    gain_own, gain_sib = two_halves(gain_parts, 1, first)
    small_own = jnp.concatenate(
        [gain_own[0, 0], gain_own[1, 0], bias_part.reshape(n_dp, -1)], axis=1
    )
    small_sib = jnp.concatenate(
        [gain_sib[0, 0], gain_sib[1, 0], bias_part.reshape(n_dp, -1)], axis=1
    )
    small = small_own + swapped(small_sib, "tr")
    split = 2 * (width // n_dp)
    gain_sum = small[:, :split]
    gain_sum = gain_sum + swapped(gain_sum, "tc")
    small = jnp.concatenate([gain_sum, small[:, split:]], axis=1)
    small = small.reshape((2,) * bits + (small.shape[1],))
    for bit in range(bits - 1, -1, -1):
        keep, send = exchange_bit(small, 0, bit)
        small = keep + swapped(send, "dp", 1 << bit)
    return (
        placed(block_out),
        placed(dx),
        d_w_qkv,
        small[split:],
        d_w_o,
        d_w_gu,
        d_w_down,
        small[: split // 2],
        small[split // 2 : split],
    )


def solution(mesh):
    placed = (
        P(("dp", "tc"), "tr"),
        P("tr"),
        P("tr", "tc"),
        P("tc"),
        P("tr", "tc"),
        P("tr"),
        P(None, "tr", "tc"),
        P("tr", "tc"),
        P(("dp", "tc"), "tr"),
    )
    return jax.shard_map(
        per_device,
        mesh=mesh,
        in_specs=placed,
        out_specs=(
            P(("dp", "tc"), "tr"),
            P(("dp", "tc"), "tr"),
            P("tr", ("tc", "dp")),
            P(("tc", "dp")),
            P("tr", ("tc", "dp")),
            P(None, "tr", ("tc", "dp")),
            P("tr", ("tc", "dp")),
            P(("tr", "dp")),
            P(("tr", "dp")),
        ),
        check_vma=False,
    )
```

```python
import jax
import jax.numpy as jnp
from jax import lax
from jax.sharding import PartitionSpec as P

QUERY_HEADS = 14
KEY_VALUE_HEADS = 2
HEAD_SIZE = 64
SEQUENCE_TOKENS = 512


EPS = 1e-06
ROPE_BASE = 1000000.0


def rotate_half(value):
    half = value.shape[-1] // 2
    return jnp.concatenate([-value[..., half:], value[..., :half]], axis=-1)


def rope_tables(positions, head_index):
    half = head_index // 2
    inverse = ROPE_BASE ** (-jnp.arange(half, dtype=jnp.float32) * 2.0 / head_index)
    angle = positions.astype(jnp.float32)[:, None] * inverse[None, :]
    angle = jnp.concatenate([angle, angle], axis=1)
    return (jnp.cos(angle), jnp.sin(angle))


def rope_apply(value, cosv, sinv):
    return value * cosv + rotate_half(value) * sinv


def rope_back(value, cosv, sinv):
    return value * cosv - rotate_half(value * sinv)


def contract_last(left, right):
    return lax.dot_general(
        left, right, (((1,), (1,)), ((), ())), preferred_element_type=jnp.float32
    )


def contract_first(left, right):
    return lax.dot_general(
        left, right, (((0,), (0,)), ((), ())), preferred_element_type=jnp.float32
    )


def swapped(values, axis, bit=1):
    size = lax.axis_size(axis)
    return lax.ppermute(values, axis, [(i, i ^ bit) for i in range(size)])


def after(value, *earlier):
    return lax.optimization_barrier((value,) + earlier)[0]


def both(values, axis, first, dim):
    return joined(values, swapped(values, axis), dim, first)


def with_rows(values, axis):
    return jnp.concatenate([values, swapped(values, axis)], axis=0)


def sum_rows(values, axis):
    rows = values.shape[0] // 2
    send = values[rows:].astype(jnp.bfloat16)
    return values[:rows].astype(jnp.float32) + swapped(send, axis).astype(jnp.float32)


def two_halves(values, axis, first):
    half = values.shape[axis] // 2
    low = lax.slice_in_dim(values, 0, half, axis=axis)
    high = lax.slice_in_dim(values, half, 2 * half, axis=axis)
    return (jnp.where(first, low, high), jnp.where(first, high, low))


def joined(mine, other, axis, first):
    return jnp.where(
        first,
        jnp.concatenate([mine, other], axis=axis),
        jnp.concatenate([other, mine], axis=axis),
    )


def exchange_bit(value, dim, bit):
    mine = lax.rem(lax.axis_index("dp") // (1 << bit), 2)
    keep = lax.dynamic_index_in_dim(value, mine, dim, keepdims=False)
    send = lax.dynamic_index_in_dim(value, 1 - mine, dim, keepdims=False)
    return (keep, send)


def scatter_begin(grad, bits, flip):
    value = grad.reshape((2,) * bits + (grad.shape[0] >> bits, grad.shape[1]))
    order = list(range(bits))
    if flip and bits > 1:
        order[0], order[1] = 1, 0
    return scatter_send(value, order, list(range(bits))[::-1])


def scatter_send(value, order, left):
    keep, send = exchange_bit(value, left.index(order[0]), order[0])
    got = swapped(send, "dp", 1 << order[0])
    return (keep, got, order[1:], [bit for bit in left if bit != order[0]])


def scatter_next(state, *earlier):
    keep, got, order, left = state
    keep = after(keep, *earlier) if earlier else keep
    value = keep.astype(jnp.float32) + got.astype(jnp.float32)
    if not order:
        return (value, None, order, left)
    return scatter_send(value.astype(jnp.bfloat16), order, left)


def scatter_rest(state):
    while state[1] is not None:
        state = scatter_next(state)
    return state[0]


def last_bit(own, other, top):
    which = (lax.axis_index("dp") // (1 << top)) == lax.axis_index("tr")
    keep = jnp.where(which, own, other)
    send = jnp.where(which, other, own).astype(jnp.bfloat16)
    return keep.astype(jnp.float32) + swapped(send, "dp", 1 << top).astype(jnp.float32)


def product(left, right):
    return contract_first(left, right).astype(jnp.bfloat16)


def attend(query, keys, values, qpos, kpos):
    scale = query.shape[-1] ** (-0.5)
    scores = jnp.einsum("tkgd,skd->kgts", query, keys, preferred_element_type=jnp.float32) * scale
    scores = jnp.where(qpos[:, None] >= kpos[None, :], scores, -1e30)
    top = jnp.max(scores, axis=3, keepdims=True)
    lse = top + jnp.log(jnp.sum(jnp.exp(scores - top), axis=3, keepdims=True))
    prob = jnp.exp(scores - lse).astype(jnp.bfloat16)
    output = jnp.einsum("kgts,skd->tkgd", prob, values, preferred_element_type=jnp.float32).astype(
        jnp.bfloat16
    )
    return (output, lse)


def attend_back(query, keys, values, output, dout, lse, qpos, kpos):
    scale = query.shape[-1] ** (-0.5)
    scores = jnp.einsum("tkgd,skd->kgts", query, keys, preferred_element_type=jnp.float32) * scale
    scores = jnp.where(qpos[:, None] >= kpos[None, :], scores, -1e30)
    prob = jnp.exp(scores - lse)
    prob_b = prob.astype(jnp.bfloat16)
    delta = jnp.transpose(
        jnp.sum(dout.astype(jnp.float32) * output.astype(jnp.float32), axis=3), (1, 2, 0)
    )[..., None]
    dprob = jnp.einsum("tkgd,skd->kgts", dout, values, preferred_element_type=jnp.float32)
    dscore = (prob * (dprob - delta) * scale).astype(jnp.bfloat16)
    dquery = jnp.einsum("kgts,skd->tkgd", dscore, keys, preferred_element_type=jnp.float32)
    dkeys = jnp.einsum("kgts,tkgd->skd", dscore, query, preferred_element_type=jnp.float32)
    dvalues = jnp.einsum("kgts,tkgd->skd", prob_b, dout, preferred_element_type=jnp.float32)
    return (dquery, dkeys, dvalues)


def per_device(
    block_in,
    g_attn,
    query_key_value_weight,
    query_key_value_bias,
    output_weight,
    g_mlp,
    w_gu,
    w_down,
    dy,
):
    f32 = jnp.float32
    bf16 = jnp.bfloat16
    n_dp = lax.axis_size("dp")
    bits = n_dp.bit_length() - 1
    first = lax.axis_index("tr") == 0
    head_group = QUERY_HEADS // KEY_VALUE_HEADS
    heads_kv = query_key_value_weight.shape[1] // ((head_group + 2) * HEAD_SIZE)
    qkv_columns = query_key_value_weight.shape[1]
    head_columns = output_weight.shape[1]
    width = block_in.shape[1]
    model_width = 2 * width
    seqs = block_in.shape[0] * 2 // SEQUENCE_TOKENS
    quarter = SEQUENCE_TOKENS // 4
    rows = seqs * quarter
    assert lax.axis_size("tr") == 2 and lax.axis_size("tc") == 2 and seqs == 1

    x_mine, x_other = two_halves(block_in, 0, first)
    x_full = joined(x_mine, swapped(x_other, "tr"), 1, first)
    gains = both(jnp.stack([g_attn, g_mlp]), "tr", first, 1)
    gain_a, gain_m = gains[0], gains[1]
    xf = x_full.astype(f32)
    r1 = lax.rsqrt(jnp.sum(xf * xf, axis=1, keepdims=True) / model_width + EPS)
    xn1 = (xf * r1 * gain_a).astype(bf16)
    w_qkv = both(query_key_value_weight, "tr", first, 0)
    w_gu, w_down, dy, output_weight = (
        after(value, xn1) for value in (w_gu, w_down, dy, output_weight)
    )
    w_o = both(output_weight, "tr", first, 0)
    dy_mine, dy_other = two_halves(dy, 0, first)
    dy_full = joined(dy_mine, swapped(dy_other, "tr"), 1, first)
    xn1_pair = with_rows(xn1, "tc")
    xn1_all = with_rows(xn1_pair, "tr")

    tr = lax.axis_index("tr")
    tc = lax.axis_index("tc")
    places = jnp.arange(quarter)
    starts = [
        tc * 2 * quarter + tr * quarter,
        (1 - tc) * 2 * quarter + tr * quarter,
        tc * 2 * quarter + (1 - tr) * quarter,
        (1 - tc) * 2 * quarter + (1 - tr) * quarter,
    ]
    kpos = jnp.concatenate([start + places for start in starts])
    qpos = kpos[: 2 * quarter]
    cosv, sinv = rope_tables(kpos, HEAD_SIZE)
    qkv = jnp.dot(xn1_all, w_qkv, preferred_element_type=f32) + query_key_value_bias
    qkv = qkv.reshape(4 * rows, heads_kv, head_group + 2, HEAD_SIZE)
    cos_q, sin_q = cosv[: 2 * rows], sinv[: 2 * rows]
    query = rope_apply(
        qkv[: 2 * rows, :, :head_group], cos_q[:, None, None], sin_q[:, None, None]
    ).astype(bf16)
    keys = rope_apply(qkv[:, :, head_group], cosv[:, None], sinv[:, None]).astype(bf16)
    values = qkv[:, :, head_group + 1].astype(bf16)
    output, lse = attend(query, keys, values, qpos, kpos)
    o_pair = output.reshape(2 * rows, head_columns)
    h1 = xf + sum_rows(contract_last(o_pair, w_o), "tc")

    gu_mine, gu_other = two_halves(w_gu, 2, first)
    wgu = joined(gu_mine, swapped(gu_other, "tr"), 1, first)
    down_mine, down_other = two_halves(w_down, 1, first)
    wdown = joined(down_mine, swapped(down_other, "tr"), 0, first)
    dy_all = with_rows(with_rows(after(dy_full, xn1_pair), "tc"), "tr")
    dmixed = jnp.dot(dy_all, wdown, preferred_element_type=f32)

    r2 = lax.rsqrt(jnp.sum(h1 * h1, axis=1, keepdims=True) / model_width + EPS)
    xn2 = (h1 * r2 * gain_m).astype(bf16)
    xn2_pair = with_rows(xn2, "tc")
    xn2_all = with_rows(after(xn2_pair, wgu, dmixed), "tr")
    gate = jnp.dot(xn2_all, wgu[0], preferred_element_type=f32)
    upper = jnp.dot(xn2_all, wgu[1], preferred_element_type=f32)
    sig = jax.nn.sigmoid(gate)
    silu_v = gate * sig
    mixed = (silu_v * upper).astype(bf16)
    dgate = (dmixed * upper * sig * (1.0 + gate * (1.0 - sig))).astype(bf16)
    dup = (dmixed * silu_v).astype(bf16)

    dy_own, dy_sib = two_halves(dy_all, 1, first)
    xn2_own, xn2_sib = two_halves(xn2_all, 1, first)
    pairs = [(mixed, dy_own, dy_sib), (dgate, xn2_own, xn2_sib), (dup, xn2_own, xn2_sib)]
    low = bits - 1

    def hidden_grad(index, *earlier):
        left, own, sib = pairs[index]
        left = after(left, *earlier) if earlier else left
        other = product(left, sib)
        return (product(left, own), other, swapped(other, "tr"))

    grad_0 = hidden_grad(0)
    own_0 = scatter_begin(grad_0[0], low, False)
    grad_1 = hidden_grad(1, *grad_0[:2])
    own_1 = scatter_begin(grad_1[0], low, False)
    other_0 = scatter_begin(grad_0[2], low, True)
    dgate, dup_chain = after((dgate, dup), grad_0[2], *grad_1[:2])
    dxn2 = contract_last(dgate, wgu[0]) + contract_last(dup_chain, wgu[1])
    grad_2 = hidden_grad(2, dxn2)
    own_2 = scatter_begin(grad_2[0], low, False)
    dxn2 = sum_rows(dxn2, "tr")
    other_1 = scatter_begin(grad_1[2], low, True)
    dxn2 = sum_rows(after(dxn2, grad_1[2], own_0[1], *grad_2[:2]), "tc")
    d_g_mlp = jnp.sum(dxn2 * h1 * r2, axis=0)
    scaled = gain_m * dxn2
    dh1 = (
        dy_full.astype(f32)
        + r2 * scaled
        - h1 * r2**3 * (jnp.sum(scaled * h1, axis=1, keepdims=True) / model_width)
    )
    dh1b = after(dh1.astype(bf16), other_0[1], own_1[1], grad_2[2])
    other_2 = scatter_begin(after(grad_2[2], dh1b), low, True)
    dh1_pair = with_rows(dh1b, "tc")
    down_next = [scatter_next(own_0, dh1b), scatter_next(other_0, dh1b)]
    mlp_out = sum_rows(contract_last(after(mixed, dh1b), wdown), "tr")
    dh1_pair = after(dh1_pair, other_1[1], mlp_out)
    gate_next = [scatter_next(own_1, dh1_pair), scatter_next(other_1, dh1_pair)]
    mlp_out = sum_rows(mlp_out, "tc")
    dout = jnp.dot(dh1_pair, w_o, preferred_element_type=f32).astype(bf16)
    dout = dout.reshape(2 * rows, heads_kv, head_group, HEAD_SIZE)
    dquery, dkeys, dvalues = attend_back(
        query, keys, values, output, dout, lse, qpos, kpos
    )
    kv_part = jnp.stack([dkeys, dvalues], axis=2).reshape(4 * rows, heads_kv * 2 * HEAD_SIZE)
    kv_back = sum_rows(kv_part, "tr").reshape(2 * rows, heads_kv, 2, HEAD_SIZE)
    q_back = rope_back(dquery, cos_q[:, None, None], sin_q[:, None, None])
    k_back = rope_back(kv_back[:, :, 0], cos_q[:, None], sin_q[:, None])
    dqkv = jnp.concatenate(
        [q_back, k_back[:, :, None], kv_back[:, :, 1][:, :, None]], axis=2
    ).reshape(2 * rows, qkv_columns)
    bias_part = jnp.sum(dqkv, axis=0)
    dqkvb = after(dqkv.astype(bf16), other_2[1], own_2[1], mlp_out)
    up_next = [scatter_next(own_2, dqkvb), scatter_next(other_2, dqkvb)]
    dxn1 = contract_last(dqkvb, w_qkv)
    dxn1 = sum_rows(after(dxn1, down_next[0][1], down_next[1][1]), "tc")

    def pair_grad(left, right, flip):
        own, sib = two_halves(right, 1, first)
        got = swapped(product(left, sib), "tr")
        total = (contract_first(left, own) + got.astype(f32)).astype(bf16)
        return scatter_rest(scatter_begin(total, bits, flip)).T

    hidden_sums = [
        last_bit(scatter_rest(own), scatter_rest(other), low).T
        for own, other in (down_next, gate_next, up_next)
    ]
    d_w_down = hidden_sums[0]
    d_w_gu = jnp.stack(hidden_sums[1:])
    d_w_qkv = pair_grad(dqkvb, xn1_pair, True)
    d_w_o = pair_grad(o_pair, dh1_pair, False)

    d_g_attn = jnp.sum(dxn1 * xf * r1, axis=0)
    scaled = gain_a * dxn1
    dx = (
        dh1
        + r1 * scaled
        - xf * r1**3 * (jnp.sum(scaled * xf, axis=1, keepdims=True) / model_width)
    )

    block_out = (h1 + mlp_out).astype(bf16)

    def placed(full):
        own, sib = two_halves(full, 1, first)
        return joined(own, swapped(sib, "tr"), 0, first)

    gain_parts = jnp.stack([d_g_attn, d_g_mlp]).reshape(2, 2, n_dp, width // n_dp)
    gain_own, gain_sib = two_halves(gain_parts, 1, first)
    small_own = jnp.concatenate(
        [gain_own[0, 0], gain_own[1, 0], bias_part.reshape(n_dp, -1)], axis=1
    )
    small_sib = jnp.concatenate(
        [gain_sib[0, 0], gain_sib[1, 0], bias_part.reshape(n_dp, -1)], axis=1
    )
    small = small_own + swapped(small_sib, "tr")
    split = 2 * (width // n_dp)
    gain_sum = small[:, :split]
    gain_sum = gain_sum + swapped(gain_sum, "tc")
    small = jnp.concatenate([gain_sum, small[:, split:]], axis=1)
    small = small.reshape((2,) * bits + (small.shape[1],))
    for bit in range(bits - 1, -1, -1):
        keep, send = exchange_bit(small, 0, bit)
        small = keep + swapped(send, "dp", 1 << bit)
    return (
        placed(block_out),
        placed(dx),
        d_w_qkv,
        small[split:],
        d_w_o,
        d_w_gu,
        d_w_down,
        small[: split // 2],
        small[split // 2 : split],
    )


def solution(mesh):
    placed = (
        P(("dp", "tc"), "tr"),
        P("tr"),
        P("tr", "tc"),
        P("tc"),
        P("tr", "tc"),
        P("tr"),
        P(None, "tr", "tc"),
        P("tr", "tc"),
        P(("dp", "tc"), "tr"),
    )
    return jax.shard_map(
        per_device,
        mesh=mesh,
        in_specs=placed,
        out_specs=(
            P(("dp", "tc"), "tr"),
            P(("dp", "tc"), "tr"),
            P("tr", ("tc", "dp")),
            P(("tc", "dp")),
            P("tr", ("tc", "dp")),
            P(None, "tr", ("tc", "dp")),
            P("tr", ("tc", "dp")),
            P(("tr", "dp")),
            P(("tr", "dp")),
        ),
        check_vma=False,
    )
```

```python
import jax
import jax.numpy as jnp
from jax import lax
from jax.sharding import PartitionSpec as P

QUERY_HEADS = 14
KEY_VALUE_HEADS = 2
HEAD_SIZE = 64
SEQUENCE_TOKENS = 512


EPS = 1e-06
ROPE_BASE = 1000000.0


def rotate_half(value):
    half = value.shape[-1] // 2
    return jnp.concatenate([-value[..., half:], value[..., :half]], axis=-1)


def rope_tables(positions, head_index):
    half = head_index // 2
    inverse = ROPE_BASE ** (-jnp.arange(half, dtype=jnp.float32) * 2.0 / head_index)
    angle = positions.astype(jnp.float32)[:, None] * inverse[None, :]
    angle = jnp.concatenate([angle, angle], axis=1)
    return (jnp.cos(angle), jnp.sin(angle))


def rope_apply(value, cosv, sinv):
    return value * cosv + rotate_half(value) * sinv


def rope_back(value, cosv, sinv):
    return value * cosv - rotate_half(value * sinv)


def contract_last(left, right):
    return lax.dot_general(
        left, right, (((1,), (1,)), ((), ())), preferred_element_type=jnp.float32
    )


def contract_first(left, right):
    return lax.dot_general(
        left, right, (((0,), (0,)), ((), ())), preferred_element_type=jnp.float32
    )


def swapped(values, axis, bit=1):
    size = lax.axis_size(axis)
    return lax.ppermute(values, axis, [(i, i ^ bit) for i in range(size)])


def after(value, *earlier):
    return lax.optimization_barrier((value,) + earlier)[0]


def both(values, axis, first, dim):
    return joined(values, swapped(values, axis), dim, first)


def with_rows(values, axis):
    return jnp.concatenate([values, swapped(values, axis)], axis=0)


def sum_rows(values, axis):
    rows = values.shape[0] // 2
    send = values[rows:].astype(jnp.bfloat16)
    return values[:rows].astype(jnp.float32) + swapped(send, axis).astype(jnp.float32)


def two_halves(values, axis, first):
    half = values.shape[axis] // 2
    low = lax.slice_in_dim(values, 0, half, axis=axis)
    high = lax.slice_in_dim(values, half, 2 * half, axis=axis)
    return (jnp.where(first, low, high), jnp.where(first, high, low))


def joined(mine, other, axis, first):
    return jnp.where(
        first,
        jnp.concatenate([mine, other], axis=axis),
        jnp.concatenate([other, mine], axis=axis),
    )


def exchange_bit(value, dim, bit):
    mine = lax.rem(lax.axis_index("dp") // (1 << bit), 2)
    keep = lax.dynamic_index_in_dim(value, mine, dim, keepdims=False)
    send = lax.dynamic_index_in_dim(value, 1 - mine, dim, keepdims=False)
    return (keep, send)


def scatter_begin(grad, bits, flip):
    value = grad.reshape((2,) * bits + (grad.shape[0] >> bits, grad.shape[1]))
    order = list(range(bits))
    if flip and bits > 1:
        order[0], order[1] = 1, 0
    return scatter_send(value, order, list(range(bits))[::-1])


def scatter_send(value, order, left):
    keep, send = exchange_bit(value, left.index(order[0]), order[0])
    got = swapped(send, "dp", 1 << order[0])
    return (keep, got, order[1:], [bit for bit in left if bit != order[0]])


def scatter_next(state, *earlier):
    keep, got, order, left = state
    keep = after(keep, *earlier) if earlier else keep
    value = keep.astype(jnp.float32) + got.astype(jnp.float32)
    if not order:
        return (value, None, order, left)
    return scatter_send(value.astype(jnp.bfloat16), order, left)


def scatter_rest(state):
    while state[1] is not None:
        state = scatter_next(state)
    return state[0]


def last_bit(own, other, top):
    which = (lax.axis_index("dp") // (1 << top)) == lax.axis_index("tr")
    keep = jnp.where(which, own, other)
    send = jnp.where(which, other, own).astype(jnp.bfloat16)
    return keep.astype(jnp.float32) + swapped(send, "dp", 1 << top).astype(jnp.float32)


def product(left, right):
    return contract_first(left, right).astype(jnp.bfloat16)


def attend(query, keys, values, qpos, kpos):
    scale = query.shape[-1] ** (-0.5)
    scores = jnp.einsum("tkgd,skd->kgts", query, keys, preferred_element_type=jnp.float32) * scale
    scores = jnp.where(qpos[:, None] >= kpos[None, :], scores, -1e30)
    top = jnp.max(scores, axis=3, keepdims=True)
    lse = top + jnp.log(jnp.sum(jnp.exp(scores - top), axis=3, keepdims=True))
    prob = jnp.exp(scores - lse).astype(jnp.bfloat16)
    output = jnp.einsum("kgts,skd->tkgd", prob, values, preferred_element_type=jnp.float32).astype(
        jnp.bfloat16
    )
    return (output, lse)


def attend_back(query, keys, values, output, dout, lse, qpos, kpos):
    scale = query.shape[-1] ** (-0.5)
    scores = jnp.einsum("tkgd,skd->kgts", query, keys, preferred_element_type=jnp.float32) * scale
    scores = jnp.where(qpos[:, None] >= kpos[None, :], scores, -1e30)
    prob = jnp.exp(scores - lse)
    prob_b = prob.astype(jnp.bfloat16)
    delta = jnp.transpose(
        jnp.sum(dout.astype(jnp.float32) * output.astype(jnp.float32), axis=3), (1, 2, 0)
    )[..., None]
    dprob = jnp.einsum("tkgd,skd->kgts", dout, values, preferred_element_type=jnp.float32)
    dscore = (prob * (dprob - delta) * scale).astype(jnp.bfloat16)
    dquery = jnp.einsum("kgts,skd->tkgd", dscore, keys, preferred_element_type=jnp.float32)
    dkeys = jnp.einsum("kgts,tkgd->skd", dscore, query, preferred_element_type=jnp.float32)
    dvalues = jnp.einsum("kgts,tkgd->skd", prob_b, dout, preferred_element_type=jnp.float32)
    return (dquery, dkeys, dvalues)


def per_device(
    block_in,
    g_attn,
    query_key_value_weight,
    query_key_value_bias,
    output_weight,
    g_mlp,
    w_gu,
    w_down,
    dy,
):
    f32 = jnp.float32
    bf16 = jnp.bfloat16
    n_dp = lax.axis_size("dp")
    bits = n_dp.bit_length() - 1
    first = lax.axis_index("tr") == 0
    head_group = QUERY_HEADS // KEY_VALUE_HEADS
    heads_kv = query_key_value_weight.shape[1] // ((head_group + 2) * HEAD_SIZE)
    qkv_columns = query_key_value_weight.shape[1]
    head_columns = output_weight.shape[1]
    width = block_in.shape[1]
    model_width = 2 * width
    seqs = block_in.shape[0] * 2 // SEQUENCE_TOKENS
    quarter = SEQUENCE_TOKENS // 4
    rows = seqs * quarter
    assert lax.axis_size("tr") == 2 and lax.axis_size("tc") == 2 and seqs == 1

    x_mine, x_other = two_halves(block_in, 0, first)
    x_full = joined(x_mine, swapped(x_other, "tr"), 1, first)
    gains = both(jnp.stack([g_attn, g_mlp]), "tr", first, 1)
    gain_a, gain_m = gains[0], gains[1]
    xf = x_full.astype(f32)
    r1 = lax.rsqrt(jnp.sum(xf * xf, axis=1, keepdims=True) / model_width + EPS)
    xn1 = (xf * r1 * gain_a).astype(bf16)
    w_qkv = both(query_key_value_weight, "tr", first, 0)
    w_gu, w_down, dy, output_weight = (
        after(value, xn1) for value in (w_gu, w_down, dy, output_weight)
    )
    w_o = both(output_weight, "tr", first, 0)
    dy_mine, dy_other = two_halves(dy, 0, first)
    dy_full = joined(dy_mine, swapped(dy_other, "tr"), 1, first)
    xn1_pair = with_rows(xn1, "tc")
    xn1_all = with_rows(xn1_pair, "tr")

    tr = lax.axis_index("tr")
    tc = lax.axis_index("tc")
    places = jnp.arange(quarter)
    starts = [
        tc * 2 * quarter + tr * quarter,
        (1 - tc) * 2 * quarter + tr * quarter,
        tc * 2 * quarter + (1 - tr) * quarter,
        (1 - tc) * 2 * quarter + (1 - tr) * quarter,
    ]
    kpos = jnp.concatenate([start + places for start in starts])
    qpos = kpos[: 2 * quarter]
    cosv, sinv = rope_tables(kpos, HEAD_SIZE)
    qkv = jnp.dot(xn1_all, w_qkv, preferred_element_type=f32) + query_key_value_bias
    qkv = qkv.reshape(4 * rows, heads_kv, head_group + 2, HEAD_SIZE)
    cos_q, sin_q = cosv[: 2 * rows], sinv[: 2 * rows]
    query = rope_apply(
        qkv[: 2 * rows, :, :head_group], cos_q[:, None, None], sin_q[:, None, None]
    ).astype(bf16)
    keys = rope_apply(qkv[:, :, head_group], cosv[:, None], sinv[:, None]).astype(bf16)
    values = qkv[:, :, head_group + 1].astype(bf16)
    output, lse = attend(query, keys, values, qpos, kpos)
    o_pair = output.reshape(2 * rows, head_columns)
    h1 = xf + sum_rows(contract_last(o_pair, w_o), "tc")

    gu_mine, gu_other = two_halves(w_gu, 2, first)
    wgu = joined(gu_mine, swapped(gu_other, "tr"), 1, first)
    down_mine, down_other = two_halves(w_down, 1, first)
    wdown = joined(down_mine, swapped(down_other, "tr"), 0, first)
    dy_all = with_rows(with_rows(after(dy_full, xn1_pair), "tc"), "tr")
    dmixed = jnp.dot(dy_all, wdown, preferred_element_type=f32)

    r2 = lax.rsqrt(jnp.sum(h1 * h1, axis=1, keepdims=True) / model_width + EPS)
    xn2 = (h1 * r2 * gain_m).astype(bf16)
    xn2_pair = with_rows(xn2, "tc")
    xn2_all = with_rows(after(xn2_pair, wgu, dmixed), "tr")
    gate = jnp.dot(xn2_all, wgu[0], preferred_element_type=f32)
    upper = jnp.dot(xn2_all, wgu[1], preferred_element_type=f32)
    sig = jax.nn.sigmoid(gate)
    silu_v = gate * sig
    mixed = (silu_v * upper).astype(bf16)
    dgate = (dmixed * upper * sig * (1.0 + gate * (1.0 - sig))).astype(bf16)
    dup = (dmixed * silu_v).astype(bf16)

    dy_own, dy_sib = two_halves(dy_all, 1, first)
    xn2_own, xn2_sib = two_halves(xn2_all, 1, first)
    pairs = [(mixed, dy_own, dy_sib), (dgate, xn2_own, xn2_sib), (dup, xn2_own, xn2_sib)]
    low = bits - 1

    def hidden_grad(index, *earlier):
        left, own, sib = pairs[index]
        left = after(left, *earlier) if earlier else left
        other = product(left, sib)
        return (product(left, own), other, swapped(other, "tr"))

    grad_0 = hidden_grad(0)
    own_0 = scatter_begin(grad_0[0], low, False)
    grad_1 = hidden_grad(1, *grad_0[:2])
    own_1 = scatter_begin(grad_1[0], low, False)
    other_0 = scatter_begin(grad_0[2], low, True)
    dgate, dup_chain = after((dgate, dup), grad_0[2], *grad_1[:2])
    dxn2 = contract_last(dgate, wgu[0]) + contract_last(dup_chain, wgu[1])
    grad_2 = hidden_grad(2, dxn2)
    own_2 = scatter_begin(grad_2[0], low, False)
    dxn2 = sum_rows(dxn2, "tr")
    other_1 = scatter_begin(grad_1[2], low, True)
    dxn2 = sum_rows(after(dxn2, grad_1[2], own_0[1], *grad_2[:2]), "tc")
    d_g_mlp = jnp.sum(dxn2 * h1 * r2, axis=0)
    scaled = gain_m * dxn2
    dh1 = (
        dy_full.astype(f32)
        + r2 * scaled
        - h1 * r2**3 * (jnp.sum(scaled * h1, axis=1, keepdims=True) / model_width)
    )
    dh1b = after(dh1.astype(bf16), other_0[1], own_1[1], grad_2[2])
    other_2 = scatter_begin(after(grad_2[2], dh1b), low, True)
    dh1_pair = with_rows(dh1b, "tc")
    down_next = [scatter_next(own_0, dh1b), scatter_next(other_0, dh1b)]
    mlp_out = sum_rows(contract_last(after(mixed, dh1b), wdown), "tr")
    dh1_pair = after(dh1_pair, other_1[1], mlp_out)
    gate_next = [scatter_next(own_1, dh1_pair), scatter_next(other_1, dh1_pair)]
    mlp_out = sum_rows(mlp_out, "tc")
    dout = jnp.dot(dh1_pair, w_o, preferred_element_type=f32).astype(bf16)
    dout = dout.reshape(2 * rows, heads_kv, head_group, HEAD_SIZE)
    dquery, dkeys, dvalues = attend_back(
        query, keys, values, output, dout, lse, qpos, kpos
    )
    kv_part = jnp.stack([dkeys, dvalues], axis=2).reshape(4 * rows, heads_kv * 2 * HEAD_SIZE)
    kv_back = sum_rows(kv_part, "tr").reshape(2 * rows, heads_kv, 2, HEAD_SIZE)
    q_back = rope_back(dquery, cos_q[:, None, None], sin_q[:, None, None])
    k_back = rope_back(kv_back[:, :, 0], cos_q[:, None], sin_q[:, None])
    dqkv = jnp.concatenate(
        [q_back, k_back[:, :, None], kv_back[:, :, 1][:, :, None]], axis=2
    ).reshape(2 * rows, qkv_columns)
    bias_part = jnp.sum(dqkv, axis=0)
    dqkvb = after(dqkv.astype(bf16), other_2[1], own_2[1])
    up_next = [scatter_next(own_2, dqkvb), scatter_next(other_2, dqkvb)]
    dh1_own, dh1_sib = two_halves(dh1_pair, 1, first)
    xn1_own, xn1_sib = two_halves(xn1_pair, 1, first)

    def attention_grad(dh1_half, xn1_half):
        grads = (contract_first(o_pair, dh1_half), contract_first(dqkvb, xn1_half))
        grads = [grad.astype(bf16).reshape(n_dp, -1, width) for grad in grads]
        return jnp.concatenate(grads, axis=1).reshape(-1, width)

    o_rows = head_columns // n_dp
    dxn1 = contract_last(dqkvb, w_qkv)
    attention_sib = attention_grad(dh1_sib, xn1_sib)
    attention_got = swapped(attention_sib, "tr")
    attention_own = attention_grad(dh1_own, xn1_own)
    dxn1 = sum_rows(after(dxn1, mlp_out), "tc")
    attention_total = (attention_own.astype(f32) + attention_got.astype(f32)).astype(bf16)
    attention_state = scatter_begin(attention_total, bits, True)
    attention_sum = scatter_rest(attention_state)

    down_next = [scatter_next(state, dout) for state in down_next]
    hidden_sums = [
        last_bit(scatter_rest(own), scatter_rest(other), low).T
        for own, other in (down_next, gate_next, up_next)
    ]
    d_w_down = hidden_sums[0]
    d_w_gu = jnp.stack(hidden_sums[1:])
    d_w_o = attention_sum[:o_rows].T
    d_w_qkv = attention_sum[o_rows:].T

    d_g_attn = jnp.sum(dxn1 * xf * r1, axis=0)
    scaled = gain_a * dxn1
    dx = (
        dh1
        + r1 * scaled
        - xf * r1**3 * (jnp.sum(scaled * xf, axis=1, keepdims=True) / model_width)
    )

    block_out = (h1 + mlp_out).astype(bf16)

    def placed(full):
        own, sib = two_halves(full, 1, first)
        return joined(own, swapped(sib, "tr"), 0, first)

    gain_parts = jnp.stack([d_g_attn, d_g_mlp]).reshape(2, 2, n_dp, width // n_dp)
    gain_own, gain_sib = two_halves(gain_parts, 1, first)
    small_own = jnp.concatenate(
        [gain_own[0, 0], gain_own[1, 0], bias_part.reshape(n_dp, -1)], axis=1
    )
    small_sib = jnp.concatenate(
        [gain_sib[0, 0], gain_sib[1, 0], bias_part.reshape(n_dp, -1)], axis=1
    )
    small = small_own + swapped(small_sib, "tr")
    split = 2 * (width // n_dp)
    gain_sum = after(small[:, :split], attention_state[0])
    gain_sum = gain_sum + swapped(gain_sum, "tc")
    small = jnp.concatenate([gain_sum, small[:, split:]], axis=1)
    small = small.reshape((2,) * bits + (small.shape[1],))
    for bit in range(bits - 1, -1, -1):
        keep, send = exchange_bit(small, 0, bit)
        small = keep + swapped(send, "dp", 1 << bit)
    return (
        placed(block_out),
        placed(dx),
        d_w_qkv,
        small[split:],
        d_w_o,
        d_w_gu,
        d_w_down,
        small[: split // 2],
        small[split // 2 : split],
    )


def solution(mesh):
    placed = (
        P(("dp", "tc"), "tr"),
        P("tr"),
        P("tr", "tc"),
        P("tc"),
        P("tr", "tc"),
        P("tr"),
        P(None, "tr", "tc"),
        P("tr", "tc"),
        P(("dp", "tc"), "tr"),
    )
    return jax.shard_map(
        per_device,
        mesh=mesh,
        in_specs=placed,
        out_specs=(
            P(("dp", "tc"), "tr"),
            P(("dp", "tc"), "tr"),
            P("tr", ("tc", "dp")),
            P(("tc", "dp")),
            P("tr", ("tc", "dp")),
            P(None, "tr", ("tc", "dp")),
            P("tr", ("tc", "dp")),
            P(("tr", "dp")),
            P(("tr", "dp")),
        ),
        check_vma=False,
    )
```
